256 devices in a mesh: col: 8 (over x_lo, y), row: 32 (over z, x_hi, core).
Axes of the slice: x: 4 (x_hi: 2, x_lo: 2; x = x_hi * 2 + x_lo), y: 4, z: 8, core: 2. Of those that a mesh axis runs over, the one named last changes fastest.
Arguments:
- upper_blocks: float32 [16384, 1024], P('row', 'col'), may hold values from -40 to 40
- lower_blocks: float32 [16384, 1024], P('row', 'col'), may hold values from -40 to 40
Outputs:
- upper_rotated: float32 [16384, 1024], P('row', 'col')
- lower_rotated: float32 [16384, 1024], P('row', 'col')
The draws below stay inside these ranges and needn't reach their ends.
All inputs are finite; a program needn't handle non-finite values.
Results may differ from the reference program's by a relative error of at most 0.0001.
Values sent between devices are 32-bit elements; how exact they have to be, the bound alone decides.
No kernel may reach another device: no remote copies, remote signals or barrier semaphores. Data moves between devices by JAX's collectives and lax.ppermute only.
A program may use at most 64 MiB of HBM per device.

```python
import math
import jax
import jax.numpy as jnp
from jax import lax

BLOCK = 128
ROUNDS = 2
HALF = 1024
COLS = 2048
ROWS = 16384
N_COL = 8


def whole_matrix(key):
    base = jax.random.fold_in(key, 11)
    keys = jax.random.split(base, 4)
    noise = jax.random.normal(keys[0], (ROWS, COLS), jnp.float32)
    mixing = jnp.eye(COLS, dtype=jnp.float32) + 0.7 * jax.random.normal(keys[1], (COLS, COLS), jnp.float32) / math.sqrt(COLS)
    mixed = jnp.dot(noise, mixing, precision=lax.Precision.HIGHEST)
    column_scale = jnp.exp(jax.random.uniform(keys[2], (COLS,), jnp.float32, math.log(0.3), math.log(3.0)))
    position = jnp.arange(ROWS, dtype=jnp.float32) / ROWS
    row_scale = jnp.exp(math.log(3.0) * position + jax.random.uniform(keys[3], (ROWS,), jnp.float32, -0.35, 0.35))
    return jnp.clip(mixed * row_scale[:, None] * column_scale[None, :] / 1.7, -40.0, 40.0)


def draw_upper_blocks(key, part):
    return whole_matrix(key)[:, :HALF]


def draw_lower_blocks(key, part):
    return whole_matrix(key)[:, HALF:]


def setup_inputs(seed: int = 0) -> dict:
    splits = jax.random.split(jax.random.key(seed), 3)
    return {
        "upper_blocks": draw_upper_blocks(jax.random.fold_in(splits[2], 71), 0),
        "lower_blocks": draw_lower_blocks(jax.random.fold_in(splits[2], 71), 0),
    }


def couple(cross_gram, upper_norms, lower_norms):
    column_gap = upper_norms[..., :, None] - lower_norms[..., None, :]
    column_sum = upper_norms[..., :, None] + lower_norms[..., None, :]
    return -cross_gram * column_gap / (2.0 * column_gap * column_gap + 0.5 * column_sum * column_sum + 1e-05)

def rotation(coupling):
    identity = jnp.eye(coupling.shape[0], dtype=coupling.dtype)
    outer_gram = jnp.dot(coupling, coupling.T, precision=lax.Precision.HIGHEST)
    inner_gram = jnp.dot(coupling.T, coupling, precision=lax.Precision.HIGHEST)
    left_factor = jnp.linalg.cholesky(identity + outer_gram)
    right_factor = jnp.linalg.cholesky(identity + inner_gram)
    keep_upper = jax.scipy.linalg.cho_solve((left_factor, True), identity - outer_gram)
    upper_to_lower = jax.scipy.linalg.cho_solve((left_factor, True), 2.0 * coupling)
    lower_to_upper = jax.scipy.linalg.cho_solve((right_factor, True), -2.0 * coupling.T)
    keep_lower = jax.scipy.linalg.cho_solve((right_factor, True), identity - inner_gram)
    return (keep_upper, upper_to_lower, lower_to_upper, keep_lower)

def reference(upper_blocks, lower_blocks):
    upper = upper_blocks.reshape(ROWS, N_COL, BLOCK)
    lower = lower_blocks.reshape(ROWS, N_COL, BLOCK)
    highest = lax.Precision.HIGHEST
    for round_index in range(ROUNDS):
        cross_gram = jnp.einsum('mcb,mcd->cbd', upper, lower, precision=highest) / ROWS
        upper_norms = jnp.sum(upper * upper, axis=0) / ROWS
        lower_norms = jnp.sum(lower * lower, axis=0) / ROWS
        coupling = couple(cross_gram, upper_norms, lower_norms)
        keep_upper, upper_to_lower, lower_to_upper, keep_lower = jax.vmap(rotation)(coupling)
        new_upper = jnp.einsum('mcb,cbd->mcd', upper, keep_upper, precision=highest) + jnp.einsum('mcb,cbd->mcd', lower, lower_to_upper, precision=highest)
        new_lower = jnp.einsum('mcb,cbd->mcd', upper, upper_to_lower, precision=highest) + jnp.einsum('mcb,cbd->mcd', lower, keep_lower, precision=highest)
        if round_index + 1 < ROUNDS:
            upper = jnp.roll(new_upper, 1, axis=1)
            lower = jnp.roll(new_lower, -1, axis=1)
        else:
            upper = new_upper
            lower = new_lower
    return (upper.reshape(ROWS, HALF), lower.reshape(ROWS, HALF))
```

```python
import functools

import jax
import jax.numpy as jnp
from jax import lax
from jax.experimental import pallas as pl
from jax.experimental.pallas import tpu as pltpu
from jax.sharding import PartitionSpec as P

ROUNDS = 2
HALF_ROWS = 72
TOLERANCE = 1e-7

Z_PAIR = {0: 1, 2: 3, 4: 5, 6: 7}
Z_FAR = ({0: 2, 1: 3, 4: 6, 5: 7}, {0: 6, 1: 7, 2: 4, 3: 5}, {0: 5, 1: 4, 2: 7, 3: 6})


def both_ways(pairs):
    return {**pairs, **{b: a for a, b in pairs.items()}}


def row_route(z_map=None, flip_x=False, flip_core=False):
    route = []
    for i in range(32):
        z, x, core = i // 4, i // 2 % 2, i % 2
        z = both_ways(z_map)[z] if z_map else z
        route.append((i, z * 4 + (x ^ flip_x) * 2 + (core ^ flip_core)))
    return route


def across(value, **kinds):
    return lax.ppermute(value, "row", row_route(**kinds))


def summed_over_chips(value):
    near = [across(value, flip_x=True), across(value, z_map=Z_PAIR), across(value, z_map=Z_PAIR, flip_x=True)]
    value = (value + near[0]) + (near[1] + near[2])
    far = [across(value, z_map=pairs) for pairs in Z_FAR]
    return (value + far[0]) + (far[1] + far[2])


def split(value):
    high = value.astype(jnp.bfloat16)
    return high, (value - high.astype(jnp.float32)).astype(jnp.bfloat16)


def contract(a, b, dims):
    (ah, al), (bh, bl) = a, b
    dot = functools.partial(lax.dot_general, dimension_numbers=(dims, ((), ())), preferred_element_type=jnp.float32)
    return dot(ah, bh) + (dot(al, bh) + dot(ah, bl))


def exact_dot(a, b, dims=((1,), (0,))):
    return lax.dot_general(
        a, b, dimension_numbers=(dims, ((), ())), precision=lax.Precision.HIGHEST, preferred_element_type=jnp.float32
    )


def statistics_kernel(upper_ref, lower_ref, keep_ref, send_ref):
    core = lax.axis_index("row") % 2
    upper, lower = upper_ref[...], lower_ref[...]
    gram = contract(split(upper), split(lower), ((0,), (0,)))
    sums = [jnp.sum((v * v).reshape(-1, 8, v.shape[1]), axis=0) for v in (upper, lower)]
    mine = core == 0
    keep_ref[:64] = jnp.where(mine, gram[:64], gram[64:])
    send_ref[:64] = jnp.where(mine, gram[64:], gram[:64])
    keep_ref[64:] = jnp.where(mine, sums[0], sums[1])
    send_ref[64:] = jnp.where(mine, sums[1], sums[0])


def statistics(upper, lower):
    half = jax.ShapeDtypeStruct((HALF_ROWS, upper.shape[1]), jnp.float32)
    vmem = pl.BlockSpec(memory_space=pltpu.VMEM)
    return pl.pallas_call(
        statistics_kernel, out_shape=(half, half), in_specs=[vmem, vmem], out_specs=(vmem, vmem), name="statistics"
    )(upper, lower)


def rotate_kernel(row_total, mine_ref, other_ref, upper_ref, lower_ref, new_upper_ref, new_lower_ref, residual_ref, inverse_ref):
    core = lax.axis_index("row") % 2
    mine, other = mine_ref[...], other_ref[...]
    first = jnp.where(core == 0, mine, other)
    second = jnp.where(core == 0, other, mine)
    width = mine.shape[1]
    scale = 1.0 / row_total
    cross_gram = jnp.concatenate([first[:64], second[:64]], axis=0) * scale
    upper_norms = jnp.sum(first[64:], axis=0, keepdims=True) * scale
    lower_norms = jnp.sum(second[64:], axis=0, keepdims=True) * scale
    upper_norms = jnp.broadcast_to(upper_norms, (width, width)).T
    gap = upper_norms - lower_norms
    both = upper_norms + lower_norms
    coupling = -cross_gram * gap / (2.0 * gap * gap + 0.5 * both * both + 1e-05)

    identity = (
        lax.broadcasted_iota(jnp.int32, (width, width), 0) == lax.broadcasted_iota(jnp.int32, (width, width), 1)
    ).astype(jnp.float32)
    outer = exact_dot(coupling, coupling, ((1,), (1,)))
    size = jnp.sqrt(jnp.sum(jnp.sum(outer * outer, axis=0, keepdims=True), axis=1, keepdims=True))
    alpha = 2.0 / (2.0 + size)
    bound = jnp.sum(size / (2.0 + size))
    residual_ref[...] = (1.0 - alpha) * identity - alpha * outer
    inverse_ref[...] = alpha * (identity + residual_ref[...])

    def factor(bound):
        residual = exact_dot(residual_ref[...], residual_ref[...])
        residual_ref[...] = residual
        inverse_ref[...] += exact_dot(inverse_ref[...], residual)
        return bound * bound

    lax.while_loop(lambda bound: bound > TOLERANCE, factor, bound * bound)

    @pl.when(bound > 0.5)
    def _():
        for _ in range(2):
            value = inverse_ref[...]
            inverse_ref[...] = value + exact_dot(value, (identity - value) - exact_dot(outer, value))

    inverse = inverse_ref[...]
    across_parts = 2.0 * exact_dot(inverse, coupling)
    upper_loss = 2.0 * exact_dot(outer, inverse)
    lower_loss = exact_dot(coupling, across_parts, ((0,), (0,)))
    change = jnp.concatenate(
        [
            jnp.concatenate([-upper_loss, across_parts], axis=1),
            jnp.concatenate([-across_parts.T, -lower_loss], axis=1),
        ],
        axis=0,
    )
    upper, lower = upper_ref[...], lower_ref[...]
    moved = contract(split(jnp.concatenate([upper, lower], axis=1)), split(change), ((1,), (0,)))
    new_upper_ref[...] = upper + moved[:, :width]
    new_lower_ref[...] = lower + moved[:, width:]


def rotated(mine, other, upper, lower, row_total):
    vmem = pl.BlockSpec(memory_space=pltpu.VMEM)
    return pl.pallas_call(
        functools.partial(rotate_kernel, row_total),
        out_shape=(jax.ShapeDtypeStruct(upper.shape, jnp.float32),) * 2,
        in_specs=[vmem] * 4,
        out_specs=(vmem, vmem),
        scratch_shapes=[pltpu.VMEM((upper.shape[1],) * 2, jnp.float32)] * 2,
        name="rotate",
    )(mine, other, upper, lower)


def from_behind(block, distance):
    devices = lax.axis_size("col")
    return lax.ppermute(block, "col", [((i - distance) % devices, i) for i in range(devices)])


def shards(upper, lower):
    row_total = float(upper.shape[0] * lax.axis_size("row"))
    for round_index in range(ROUNDS):
        keep, send = statistics(upper, lower)
        mine = summed_over_chips(keep + across(send, flip_core=True))
        other = across(mine, flip_core=True)
        upper, lower = rotated(mine, other, upper, lower, row_total)
        if round_index + 1 < ROUNDS:
            upper, lower = from_behind(upper, 1), from_behind(lower, -1)
    return upper, lower


def solution(mesh):
    placed = (P("row", "col"), P("row", "col"))
    return jax.shard_map(shards, mesh=mesh, in_specs=placed, out_specs=placed, check_vma=False)
```

```python
import functools

import jax
import jax.numpy as jnp
from jax import lax
from jax.experimental import pallas as pl
from jax.experimental.pallas import tpu as pltpu
from jax.sharding import PartitionSpec as P

ROUNDS = 2
FIRST_LIMIT = 56_400_000
HALF_ROWS = 72
TOLERANCE = 1e-7

Z_PAIR = {0: 1, 2: 3, 4: 5, 6: 7}
Z_FAR = ({0: 2, 1: 3, 4: 6, 5: 7}, {0: 6, 1: 7, 2: 4, 3: 5}, {0: 5, 1: 4, 2: 7, 3: 6})


def both_ways(pairs):
    return {**pairs, **{b: a for a, b in pairs.items()}}


def row_route(z_map=None, flip_x=False, flip_core=False):
    route = []
    for i in range(32):
        z, x, core = i // 4, i // 2 % 2, i % 2
        z = both_ways(z_map)[z] if z_map else z
        route.append((i, z * 4 + (x ^ flip_x) * 2 + (core ^ flip_core)))
    return route


def across(value, **kinds):
    return lax.ppermute(value, "row", row_route(**kinds))


def summed_over_chips(value):
    near = [across(value, flip_x=True), across(value, z_map=Z_PAIR), across(value, z_map=Z_PAIR, flip_x=True)]
    value = (value + near[0]) + (near[1] + near[2])
    far = [across(value, z_map=pairs) for pairs in Z_FAR]
    return (value + far[0]) + (far[1] + far[2])


def split(value):
    high = value.astype(jnp.bfloat16)
    return high, (value - high.astype(jnp.float32)).astype(jnp.bfloat16)


def contract(a, b, dims):
    (ah, al), (bh, bl) = a, b
    dot = functools.partial(lax.dot_general, dimension_numbers=(dims, ((), ())), preferred_element_type=jnp.float32)
    return dot(ah, bh) + (dot(al, bh) + dot(ah, bl))


def exact_dot(a, b, dims=((1,), (0,))):
    return lax.dot_general(
        a, b, dimension_numbers=(dims, ((), ())), precision=lax.Precision.HIGHEST, preferred_element_type=jnp.float32
    )


def write_statistics(upper, lower, keep_ref, send_ref):
    core = lax.axis_index("row") % 2
    gram = contract(split(upper), split(lower), ((0,), (0,)))
    sums = [jnp.sum((v * v).reshape(-1, 8, v.shape[1]), axis=0) for v in (upper, lower)]
    mine = core == 0
    keep_ref[:64] = jnp.where(mine, gram[:64], gram[64:])
    send_ref[:64] = jnp.where(mine, gram[64:], gram[:64])
    keep_ref[64:] = jnp.where(mine, sums[0], sums[1])
    send_ref[64:] = jnp.where(mine, sums[1], sums[0])


VMEM = pl.BlockSpec(memory_space=pltpu.VMEM)
HBM = pl.BlockSpec(memory_space=pltpu.HBM)
PARAMS = pltpu.CompilerParams(vmem_limit_bytes=8 << 20)
PIECES = 4


def pieces_of(rows):
    return [pl.ds(i * (rows // PIECES), rows // PIECES) for i in range(PIECES)]


def halves(width):
    return (jax.ShapeDtypeStruct((HALF_ROWS, width), jnp.float32),) * 2


def first_kernel(upper_hbm, lower_hbm, keep_ref, send_ref, upper_ref, lower_ref, sems):
    copies = [
        pltpu.make_async_copy(source.at[rows], target.at[rows], sems.at[i, j])
        for j, rows in enumerate(pieces_of(upper_hbm.shape[0]))
        for i, (source, target) in enumerate(((upper_hbm, upper_ref), (lower_hbm, lower_ref)))
    ]
    for copy in copies:
        copy.start()
    for copy in copies:
        copy.wait()
    write_statistics(upper_ref[...], lower_ref[...], keep_ref, send_ref)


def first_statistics(upper, lower):
    return pl.pallas_call(
        first_kernel,
        out_shape=halves(upper.shape[1]),
        in_specs=[HBM, HBM],
        out_specs=(VMEM, VMEM),
        scratch_shapes=[pltpu.VMEM(upper.shape, jnp.float32)] * 2 + [pltpu.SemaphoreType.DMA((2, PIECES))],
        compiler_params=pltpu.CompilerParams(vmem_limit_bytes=FIRST_LIMIT),
        name="first_statistics",
    )(upper, lower)


def statistics_kernel(upper_ref, lower_ref, keep_ref, send_ref):
    write_statistics(upper_ref[...], lower_ref[...], keep_ref, send_ref)


def statistics(upper, lower):
    return pl.pallas_call(
        statistics_kernel,
        out_shape=halves(upper.shape[1]),
        in_specs=[VMEM, VMEM],
        out_specs=(VMEM, VMEM),
        compiler_params=PARAMS,
        name="statistics",
    )(upper, lower)


def coupling_of(mine, other, row_total):
    core = lax.axis_index("row") % 2
    first = jnp.where(core == 0, mine, other)
    second = jnp.where(core == 0, other, mine)
    width = mine.shape[1]
    scale = 1.0 / row_total
    cross_gram = jnp.concatenate([first[:64], second[:64]], axis=0) * scale
    upper_norms = jnp.sum(first[64:], axis=0, keepdims=True) * scale
    lower_norms = jnp.sum(second[64:], axis=0, keepdims=True) * scale
    upper_norms = jnp.broadcast_to(upper_norms, (width, width)).T
    gap = upper_norms - lower_norms
    both = upper_norms + lower_norms
    return -cross_gram * gap / (2.0 * gap * gap + 0.5 * both * both + 1e-05)


def solved(coupling, residual_ref, result_ref):
    width = coupling.shape[0]
    identity = (
        lax.broadcasted_iota(jnp.int32, (width, width), 0) == lax.broadcasted_iota(jnp.int32, (width, width), 1)
    ).astype(jnp.float32)
    outer = exact_dot(coupling, coupling, ((1,), (1,)))
    size = jnp.sqrt(jnp.sum(jnp.sum(outer * outer, axis=0, keepdims=True), axis=1, keepdims=True))
    alpha = 2.0 / (2.0 + size)
    bound = jnp.sum(size / (2.0 + size))
    start = (1.0 - alpha) * identity - alpha * outer

    def factor(bound):
        residual = residual_ref[...]
        result = result_ref[...]
        result_ref[...] = result + exact_dot(residual, result)
        residual_ref[...] = exact_dot(residual, residual)
        return bound * bound

    def series(right):
        residual_ref[...] = start
        result_ref[...] = right
        lax.while_loop(lambda bound: bound > TOLERANCE, factor, bound)

    series((2.0 * alpha) * coupling)

    @pl.when(bound > 0.5)
    def _():
        for _ in range(2):
            value = result_ref[...]
            series(alpha * ((2.0 * coupling - value) - exact_dot(outer, value)))
            result_ref[...] += value

    return result_ref[...]


def change_of(mine, other, row_total, residual_ref, result_ref):
    coupling = coupling_of(mine, other, row_total)
    to_lower = solved(coupling, residual_ref, result_ref)
    upper_loss = exact_dot(coupling, to_lower, ((1,), (1,)))
    lower_loss = exact_dot(coupling, to_lower, ((0,), (0,)))
    return split(
        jnp.concatenate(
            [
                jnp.concatenate([-upper_loss, to_lower], axis=1),
                jnp.concatenate([-to_lower.T, -lower_loss], axis=1),
            ],
            axis=0,
        )
    )


def apply(upper, lower, change):
    width = upper.shape[1]
    moved = contract(split(jnp.concatenate([upper, lower], axis=1)), change, ((1,), (0,)))
    return upper + moved[:, :width], lower + moved[:, width:]


def rotate_kernel(row_total, mine_ref, other_ref, upper_ref, lower_ref, new_upper_ref, new_lower_ref, residual_ref, result_ref):
    change = change_of(mine_ref[...], other_ref[...], row_total, residual_ref, result_ref)
    new_upper_ref[...], new_lower_ref[...] = apply(upper_ref[...], lower_ref[...], change)


def last_kernel(row_total, mine_ref, other_ref, upper_ref, lower_ref, upper_hbm, lower_hbm, residual_ref, result_ref,
                new_upper_ref, new_lower_ref, sems):
    change = change_of(mine_ref[...], other_ref[...], row_total, residual_ref, result_ref)
    copies = []
    for j, rows in enumerate(pieces_of(upper_ref.shape[0])):
        new_upper_ref[rows], new_lower_ref[rows] = apply(upper_ref[rows], lower_ref[rows], change)
        for i, (source, target) in enumerate(((new_upper_ref, upper_hbm), (new_lower_ref, lower_hbm))):
            copies.append(pltpu.make_async_copy(source.at[rows], target.at[rows], sems.at[i, j]))
            copies[-1].start()
    for copy in copies:
        copy.wait()


def rotated(mine, other, upper, lower, row_total, last):
    square = pltpu.VMEM((upper.shape[1],) * 2, jnp.float32)
    scratch = [square, square]
    if last:
        scratch += [pltpu.VMEM(upper.shape, jnp.float32)] * 2 + [pltpu.SemaphoreType.DMA((2, PIECES))]
    return pl.pallas_call(
        functools.partial(last_kernel if last else rotate_kernel, row_total),
        out_shape=(jax.ShapeDtypeStruct(upper.shape, jnp.float32),) * 2,
        in_specs=[VMEM] * 4,
        out_specs=(HBM, HBM) if last else (VMEM, VMEM),
        scratch_shapes=scratch,
        compiler_params=PARAMS,
        name="rotate_last" if last else "rotate",
    )(mine, other, upper, lower)


def from_behind(block, distance):
    devices = lax.axis_size("col")
    return lax.ppermute(block, "col", [((i - distance) % devices, i) for i in range(devices)])


def shards(upper, lower):
    row_total = float(upper.shape[0] * lax.axis_size("row"))
    for round_index in range(ROUNDS):
        keep, send = statistics(upper, lower) if round_index else first_statistics(upper, lower)
        mine = summed_over_chips(keep + across(send, flip_core=True))
        other = across(mine, flip_core=True)
        last = round_index + 1 == ROUNDS
        upper, lower = rotated(mine, other, upper, lower, row_total, last)
        if not last:
            upper, lower = from_behind(upper, 1), from_behind(lower, -1)
    return upper, lower


def solution(mesh):
    placed = (P("row", "col"), P("row", "col"))
    return jax.shard_map(shards, mesh=mesh, in_specs=placed, out_specs=placed, check_vma=False)
```

```python
import functools

import jax
import jax.numpy as jnp
from jax import lax
from jax.experimental import pallas as pl
from jax.experimental.pallas import tpu as pltpu
from jax.sharding import PartitionSpec as P

ROUNDS = 2
FIRST_LIMIT = 56_400_000
STAT_ROWS = 144
TOLERANCE = 1e-7

Z_PAIR = {0: 1, 2: 3, 4: 5, 6: 7}
Z_FAR = ({0: 5, 1: 4, 2: 7, 3: 6}, {0: 2, 1: 3, 4: 6, 5: 7}, {0: 6, 1: 7, 2: 4, 3: 5})


def both_ways(pairs):
    return {**pairs, **{b: a for a, b in pairs.items()}}


def row_route(z_map=None, flip_x=False, flip_core=False):
    route = []
    for i in range(32):
        z, x, core = i // 4, i // 2 % 2, i % 2
        z = both_ways(z_map)[z] if z_map else z
        route.append((i, z * 4 + (x ^ flip_x) * 2 + (core ^ flip_core)))
    return route


def across(value, **kinds):
    return lax.ppermute(value, "row", row_route(**kinds))


def on_core_0(value, otherwise):
    return jnp.where(lax.axis_index("row") % 2 == 0, value, otherwise)


def from_three(value, single, first, second):
    route = [r for r in row_route(**single) if r[0] % 2 == 0] + [r for r in row_route(**first) if r[0] % 2]
    added = lax.ppermute(value, "row", route)
    more = lax.ppermute(value, "row", [r for r in row_route(**second) if r[0] % 2])
    return on_core_0(value, more) + added


def with_other_core(value):
    return value + across(value, flip_core=True)


def summed_over_rows(value):
    value = with_other_core(value)
    value = from_three(value, dict(z_map=Z_PAIR, flip_x=True), dict(flip_x=True), dict(z_map=Z_PAIR))
    value = with_other_core(value)
    value = from_three(value, *(dict(z_map=pairs) for pairs in Z_FAR))
    return value, across(value, flip_core=True)


def split(value):
    high = value.astype(jnp.bfloat16)
    return high, (value - high.astype(jnp.float32)).astype(jnp.bfloat16)


def contract(a, b, dims):
    (ah, al), (bh, bl) = a, b
    dot = functools.partial(lax.dot_general, dimension_numbers=(dims, ((), ())), preferred_element_type=jnp.float32)
    return dot(ah, bh) + (dot(al, bh) + dot(ah, bl))


def exact_dot(a, b, dims=((1,), (0,))):
    return lax.dot_general(
        a, b, dimension_numbers=(dims, ((), ())), precision=lax.Precision.HIGHEST, preferred_element_type=jnp.float32
    )


def write_statistics(upper, lower, out_ref):
    width = upper.shape[1]
    out_ref[:width] = contract(split(upper), split(lower), ((0,), (0,)))
    for i, value in enumerate((upper, lower)):
        out_ref[pl.ds(width + 8 * i, 8)] = jnp.sum((value * value).reshape(-1, 8, width), axis=0)


VMEM = pl.BlockSpec(memory_space=pltpu.VMEM)
HBM = pl.BlockSpec(memory_space=pltpu.HBM)
PARAMS = pltpu.CompilerParams(vmem_limit_bytes=8 << 20)
PIECES = 4


def pieces_of(rows):
    return [pl.ds(i * (rows // PIECES), rows // PIECES) for i in range(PIECES)]


def stat_shape(width):
    return jax.ShapeDtypeStruct((STAT_ROWS, width), jnp.float32)


def first_kernel(upper_hbm, lower_hbm, sums_ref, upper_ref, lower_ref, sems):
    copies = [
        pltpu.make_async_copy(source.at[rows], target.at[rows], sems.at[i, j])
        for j, rows in enumerate(pieces_of(upper_hbm.shape[0]))
        for i, (source, target) in enumerate(((upper_hbm, upper_ref), (lower_hbm, lower_ref)))
    ]
    for copy in copies:
        copy.start()
    for copy in copies:
        copy.wait()
    write_statistics(upper_ref[...], lower_ref[...], sums_ref)


def first_statistics(upper, lower):
    return pl.pallas_call(
        first_kernel,
        out_shape=stat_shape(upper.shape[1]),
        in_specs=[HBM, HBM],
        out_specs=VMEM,
        scratch_shapes=[pltpu.VMEM(upper.shape, jnp.float32)] * 2 + [pltpu.SemaphoreType.DMA((2, PIECES))],
        compiler_params=pltpu.CompilerParams(vmem_limit_bytes=FIRST_LIMIT),
        name="first_statistics",
    )(upper, lower)


def statistics_kernel(upper_ref, lower_ref, sums_ref):
    write_statistics(upper_ref[...], lower_ref[...], sums_ref)


def statistics(upper, lower):
    return pl.pallas_call(
        statistics_kernel,
        out_shape=stat_shape(upper.shape[1]),
        in_specs=[VMEM, VMEM],
        out_specs=VMEM,
        compiler_params=PARAMS,
        name="statistics",
    )(upper, lower)


def coupling_of(sums, row_total):
    width = sums.shape[1]
    sums = sums * (1.0 / row_total)
    cross_gram = sums[:width]
    upper_norms = jnp.sum(sums[width : width + 8], axis=0, keepdims=True)
    lower_norms = jnp.sum(sums[width + 8 :], axis=0, keepdims=True)
    upper_norms = jnp.broadcast_to(upper_norms, (width, width)).T
    gap = upper_norms - lower_norms
    both = upper_norms + lower_norms
    return -cross_gram * gap / (2.0 * gap * gap + 0.5 * both * both + 1e-05)


def solved(coupling, residual_ref, result_ref):
    width = coupling.shape[0]
    identity = (
        lax.broadcasted_iota(jnp.int32, (width, width), 0) == lax.broadcasted_iota(jnp.int32, (width, width), 1)
    ).astype(jnp.float32)
    parts = split(coupling)
    outer = contract(parts, parts, ((1,), (1,)))
    size = jnp.sqrt(jnp.sum(jnp.sum(outer * outer, axis=0, keepdims=True), axis=1, keepdims=True))
    alpha = 2.0 / (2.0 + size)
    bound = jnp.sum(size / (2.0 + size))
    residual = (1.0 - alpha) * identity - alpha * outer

    def series(right):
        parts = split(residual)
        right = right + contract(parts, split(right), ((1,), (0,)))
        square = contract(parts, parts, ((1,), (0,)))
        residual_ref[...] = square
        result_ref[...] = right + contract(split(square), split(right), ((1,), (0,)))

        def factor(bound):
            square = exact_dot(residual_ref[...], residual_ref[...])
            residual_ref[...] = square
            result_ref[...] += exact_dot(square, result_ref[...])
            return bound * bound

        lax.while_loop(lambda bound: bound > TOLERANCE, factor, (bound * bound) * (bound * bound))

    series((2.0 * alpha) * coupling)

    @pl.when(bound > 0.5)
    def _():
        exact_outer = exact_dot(coupling, coupling, ((1,), (1,)))
        for _ in range(2):
            value = result_ref[...]
            series(alpha * ((2.0 * coupling - value) - exact_dot(exact_outer, value)))
            result_ref[...] += value

    return result_ref[...]


def apply(upper, lower, change):
    return contract(split(jnp.concatenate([upper, lower], axis=1)), change, ((1,), (0,)))


def full_change(coupling, to_lower):
    both = (split(coupling), split(to_lower))
    upper_loss = contract(*both, ((1,), (1,)))
    lower_loss = contract(*both, ((0,), (0,)))
    return split(
        jnp.concatenate(
            [
                jnp.concatenate([-upper_loss, to_lower], axis=1),
                jnp.concatenate([-to_lower.T, -lower_loss], axis=1),
            ],
            axis=0,
        )
    )


def last_kernel(row_total, mine_ref, other_ref, upper_ref, lower_ref, upper_hbm, lower_hbm, residual_ref, result_ref,
                new_upper_ref, new_lower_ref, sems):
    coupling = coupling_of(mine_ref[...] + other_ref[...], row_total)
    to_lower = solved(coupling, residual_ref, result_ref)
    change = full_change(coupling, to_lower)
    width = upper_ref.shape[1]
    copies = []
    for j, rows in enumerate(pieces_of(upper_ref.shape[0])):
        moved = apply(upper_ref[rows], lower_ref[rows], change)
        new_upper_ref[rows] = upper_ref[rows] + moved[:, :width]
        new_lower_ref[rows] = lower_ref[rows] + moved[:, width:]
        for i, (source, target) in enumerate(((new_upper_ref, upper_hbm), (new_lower_ref, lower_hbm))):
            copies.append(pltpu.make_async_copy(source.at[rows], target.at[rows], sems.at[i, j]))
            copies[-1].start()
    for copy in copies:
        copy.wait()


def rotated_last(mine, other, upper, lower, row_total):
    width = upper.shape[1]
    square = pltpu.VMEM((width, width), jnp.float32)
    return pl.pallas_call(
        functools.partial(last_kernel, row_total),
        out_shape=(jax.ShapeDtypeStruct(upper.shape, jnp.float32),) * 2,
        in_specs=[VMEM] * 4,
        out_specs=(HBM, HBM),
        scratch_shapes=[square, square]
        + [pltpu.VMEM(upper.shape, jnp.float32)] * 2
        + [pltpu.SemaphoreType.DMA((2, PIECES))],
        compiler_params=PARAMS,
        name="rotate_last",
    )(mine, other, upper, lower)


def rotate_kernel(row_total, mine_ref, other_ref, upper_ref, lower_ref, new_upper_ref, new_lower_ref, residual_ref, result_ref):
    coupling = coupling_of(mine_ref[...] + other_ref[...], row_total)
    to_lower = solved(coupling, residual_ref, result_ref)
    width = upper_ref.shape[1]
    moved = apply(upper_ref[...], lower_ref[...], full_change(coupling, to_lower))
    new_upper_ref[...] = upper_ref[...] + moved[:, :width]
    new_lower_ref[...] = lower_ref[...] + moved[:, width:]


def rotated(mine, other, upper, lower, row_total):
    width = upper.shape[1]
    return pl.pallas_call(
        functools.partial(rotate_kernel, row_total),
        out_shape=(jax.ShapeDtypeStruct(upper.shape, jnp.float32),) * 2,
        in_specs=[VMEM] * 4,
        out_specs=(VMEM, VMEM),
        scratch_shapes=[pltpu.VMEM((width, width), jnp.float32)] * 2,
        compiler_params=PARAMS,
        name="rotate",
    )(mine, other, upper, lower)


def from_behind(block, distance):
    devices = lax.axis_size("col")
    return lax.ppermute(block, "col", [((i - distance) % devices, i) for i in range(devices)])


def shards(upper, lower):
    row_total = float(upper.shape[0] * lax.axis_size("row"))
    mine, other = summed_over_rows(first_statistics(upper, lower))
    upper, lower = rotated(mine, other, upper, lower, row_total)
    upper, lower = from_behind(upper, 1), from_behind(lower, -1)
    mine, other = summed_over_rows(statistics(upper, lower))
    return rotated_last(mine, other, upper, lower, row_total)


def solution(mesh):
    placed = (P("row", "col"), P("row", "col"))
    return jax.shard_map(shards, mesh=mesh, in_specs=placed, out_specs=placed, check_vma=False)
```

```python
import functools

import jax
import jax.numpy as jnp
from jax import lax
from jax.experimental import pallas as pl
from jax.experimental.pallas import tpu as pltpu
from jax.sharding import PartitionSpec as P

ROUNDS = 2
FIRST_LIMIT = 56_400_000
STAT_ROWS = 136
TOLERANCE = 1e-7

Z_PAIR = {0: 1, 2: 3, 4: 5, 6: 7}
Z_FAR = ({0: 5, 1: 4, 2: 7, 3: 6}, {0: 2, 1: 3, 4: 6, 5: 7}, {0: 6, 1: 7, 2: 4, 3: 5})


def both_ways(pairs):
    return {**pairs, **{b: a for a, b in pairs.items()}}


def row_route(z_map=None, flip_x=False, flip_core=False):
    route = []
    for i in range(32):
        z, x, core = i // 4, i // 2 % 2, i % 2
        z = both_ways(z_map)[z] if z_map else z
        route.append((i, z * 4 + (x ^ flip_x) * 2 + (core ^ flip_core)))
    return route


def across(value, **kinds):
    return lax.ppermute(value, "row", row_route(**kinds))


def on_core_0(value, otherwise):
    return jnp.where(lax.axis_index("row") % 2 == 0, value, otherwise)


def from_three(value, single, first, second):
    route = [r for r in row_route(**single) if r[0] % 2 == 0] + [r for r in row_route(**first) if r[0] % 2]
    added = lax.ppermute(value, "row", route)
    more = lax.ppermute(value, "row", [r for r in row_route(**second) if r[0] % 2])
    return on_core_0(value, more) + added


def with_other_core(value):
    return value + across(value, flip_core=True)


def summed_over_rows(value):
    value = with_other_core(value)
    value = from_three(value, *(dict(z_map=pairs) for pairs in Z_FAR))
    value = with_other_core(value)
    value = from_three(value, dict(z_map=Z_PAIR, flip_x=True), dict(flip_x=True), dict(z_map=Z_PAIR))
    return value, across(value, flip_core=True)


def split(value):
    high = value.astype(jnp.bfloat16)
    return high, (value - high.astype(jnp.float32)).astype(jnp.bfloat16)


def contract(a, b, dims):
    (ah, al), (bh, bl) = a, b
    dot = functools.partial(lax.dot_general, dimension_numbers=(dims, ((), ())), preferred_element_type=jnp.float32)
    return dot(ah, bh) + (dot(al, bh) + dot(ah, bl))


def exact_dot(a, b, dims=((1,), (0,))):
    return lax.dot_general(
        a, b, dimension_numbers=(dims, ((), ())), precision=lax.Precision.HIGHEST, preferred_element_type=jnp.float32
    )


def partial_statistics(upper, lower):
    squares = [jnp.sum((v * v).reshape(-1, 8, v.shape[1]), axis=0) for v in (upper, lower)]
    return [contract(split(upper), split(lower), ((0,), (0,))), *squares]


def write_statistics(parts, out_ref):
    gram, *squares = parts
    width = gram.shape[0]
    out_ref[:width] = gram
    sums = [jnp.broadcast_to(jnp.sum(s, axis=0, keepdims=True), s.shape) for s in squares]
    is_upper = lax.broadcasted_iota(jnp.int32, sums[0].shape, 0) < 4
    out_ref[width:] = jnp.where(is_upper, *sums)


VMEM = pl.BlockSpec(memory_space=pltpu.VMEM)
HBM = pl.BlockSpec(memory_space=pltpu.HBM)
PARAMS = pltpu.CompilerParams(vmem_limit_bytes=8 << 20)
PIECES = 4


def pieces_of(rows):
    return [pl.ds(i * (rows // PIECES), rows // PIECES) for i in range(PIECES)]


def stat_shape(width):
    return jax.ShapeDtypeStruct((STAT_ROWS, width), jnp.float32)


def first_kernel(upper_hbm, lower_hbm, sums_ref, upper_ref, lower_ref, sems):
    copies = [
        pltpu.make_async_copy(source.at[rows], target.at[rows], sems.at[i, j])
        for j, rows in enumerate(pieces_of(upper_hbm.shape[0]))
        for i, (source, target) in enumerate(((upper_hbm, upper_ref), (lower_hbm, lower_ref)))
    ]
    for copy in copies:
        copy.start()
    for copy in copies:
        copy.wait()
    write_statistics(partial_statistics(upper_ref[...], lower_ref[...]), sums_ref)


def first_statistics(upper, lower):
    return pl.pallas_call(
        first_kernel,
        out_shape=stat_shape(upper.shape[1]),
        in_specs=[HBM, HBM],
        out_specs=VMEM,
        scratch_shapes=[pltpu.VMEM(upper.shape, jnp.float32)] * 2 + [pltpu.SemaphoreType.DMA((2, PIECES))],
        compiler_params=pltpu.CompilerParams(vmem_limit_bytes=FIRST_LIMIT),
        name="first_statistics",
    )(upper, lower)


def statistics_kernel(upper_ref, lower_ref, sums_ref):
    write_statistics(partial_statistics(upper_ref[...], lower_ref[...]), sums_ref)


def statistics(upper, lower):
    return pl.pallas_call(
        statistics_kernel,
        out_shape=stat_shape(upper.shape[1]),
        in_specs=[VMEM, VMEM],
        out_specs=VMEM,
        compiler_params=PARAMS,
        name="statistics",
    )(upper, lower)


def coupling_of(sums, row_total):
    width = sums.shape[1]
    sums = sums * (1.0 / row_total)
    cross_gram = sums[:width]
    upper_norms, lower_norms = sums[width : width + 1], sums[width + 4 : width + 5]
    upper_norms = jnp.broadcast_to(upper_norms, (width, width)).T
    gap = upper_norms - lower_norms
    both = upper_norms + lower_norms
    return -cross_gram * gap / (2.0 * gap * gap + 0.5 * both * both + 1e-05)


def solved(coupling, residual_ref, result_ref):
    width = coupling.shape[0]
    identity = (
        lax.broadcasted_iota(jnp.int32, (width, width), 0) == lax.broadcasted_iota(jnp.int32, (width, width), 1)
    ).astype(jnp.float32)
    parts = split(coupling)
    outer = contract(parts, parts, ((1,), (1,)))
    size = jnp.sqrt(jnp.sum(jnp.sum(outer * outer, axis=0, keepdims=True), axis=1, keepdims=True))
    alpha = 2.0 / (2.0 + size)
    bound = jnp.sum(size / (2.0 + size))
    residual = (1.0 - alpha) * identity - alpha * outer

    def series(right):
        parts = split(residual)
        right = right + contract(parts, split(right), ((1,), (0,)))
        square = contract(parts, parts, ((1,), (0,)))
        residual_ref[...] = square
        result_ref[...] = right + contract(split(square), split(right), ((1,), (0,)))

        def factor(bound):
            square = exact_dot(residual_ref[...], residual_ref[...])
            residual_ref[...] = square
            result_ref[...] += exact_dot(square, result_ref[...])
            return bound * bound

        lax.while_loop(lambda bound: bound > TOLERANCE, factor, (bound * bound) * (bound * bound))

    series((2.0 * alpha) * coupling)

    @pl.when(bound > 0.5)
    def _():
        exact_outer = exact_dot(coupling, coupling, ((1,), (1,)))
        for _ in range(2):
            value = result_ref[...]
            series(alpha * ((2.0 * coupling - value) - exact_dot(exact_outer, value)))
            result_ref[...] += value

    return result_ref[...]


def apply(upper, lower, change):
    return contract(split(jnp.concatenate([upper, lower], axis=1)), change, ((1,), (0,)))


def full_change(coupling, to_lower):
    both = (split(coupling), split(to_lower))
    upper_loss = contract(*both, ((1,), (1,)))
    lower_loss = contract(*both, ((0,), (0,)))
    return split(
        jnp.concatenate(
            [
                jnp.concatenate([-upper_loss, to_lower], axis=1),
                jnp.concatenate([-to_lower.T, -lower_loss], axis=1),
            ],
            axis=0,
        )
    )


def last_kernel(row_total, mine_ref, other_ref, upper_ref, lower_ref, upper_hbm, lower_hbm, residual_ref, result_ref,
                new_upper_ref, new_lower_ref, sems):
    coupling = coupling_of(mine_ref[...] + other_ref[...], row_total)
    to_lower = solved(coupling, residual_ref, result_ref)
    change = full_change(coupling, to_lower)
    width = upper_ref.shape[1]
    copies = []
    for j, rows in enumerate(pieces_of(upper_ref.shape[0])):
        moved = apply(upper_ref[rows], lower_ref[rows], change)
        new_upper_ref[rows] = upper_ref[rows] + moved[:, :width]
        new_lower_ref[rows] = lower_ref[rows] + moved[:, width:]
        for i, (source, target) in enumerate(((new_upper_ref, upper_hbm), (new_lower_ref, lower_hbm))):
            copies.append(pltpu.make_async_copy(source.at[rows], target.at[rows], sems.at[i, j]))
            copies[-1].start()
    for copy in copies:
        copy.wait()


def rotated_last(mine, other, upper, lower, row_total):
    width = upper.shape[1]
    square = pltpu.VMEM((width, width), jnp.float32)
    return pl.pallas_call(
        functools.partial(last_kernel, row_total),
        out_shape=(jax.ShapeDtypeStruct(upper.shape, jnp.float32),) * 2,
        in_specs=[VMEM] * 4,
        out_specs=(HBM, HBM),
        scratch_shapes=[square, square]
        + [pltpu.VMEM(upper.shape, jnp.float32)] * 2
        + [pltpu.SemaphoreType.DMA((2, PIECES))],
        compiler_params=PARAMS,
        name="rotate_last",
    )(mine, other, upper, lower)


def rotate_kernel(row_total, mine_ref, other_ref, upper_ref, lower_ref, new_upper_ref, new_lower_ref, residual_ref, result_ref):
    coupling = coupling_of(mine_ref[...] + other_ref[...], row_total)
    to_lower = solved(coupling, residual_ref, result_ref)
    width = upper_ref.shape[1]
    moved = apply(upper_ref[...], lower_ref[...], full_change(coupling, to_lower))
    new_upper_ref[...] = upper_ref[...] + moved[:, :width]
    new_lower_ref[...] = lower_ref[...] + moved[:, width:]


def rotated(mine, other, upper, lower, row_total):
    width = upper.shape[1]
    return pl.pallas_call(
        functools.partial(rotate_kernel, row_total),
        out_shape=(jax.ShapeDtypeStruct(upper.shape, jnp.float32),) * 2,
        in_specs=[VMEM] * 4,
        out_specs=(VMEM, VMEM),
        scratch_shapes=[pltpu.VMEM((width, width), jnp.float32)] * 2,
        compiler_params=PARAMS,
        name="rotate",
    )(mine, other, upper, lower)


def from_behind(block, distance):
    devices = lax.axis_size("col")
    return lax.ppermute(block, "col", [((i - distance) % devices, i) for i in range(devices)])


def shards(upper, lower):
    row_total = float(upper.shape[0] * lax.axis_size("row"))
    mine, other = summed_over_rows(first_statistics(upper, lower))
    upper, lower = rotated(mine, other, upper, lower, row_total)
    upper, lower = from_behind(upper, 1), from_behind(lower, -1)
    mine, other = summed_over_rows(statistics(upper, lower))
    return rotated_last(mine, other, upper, lower, row_total)


def solution(mesh):
    placed = (P("row", "col"), P("row", "col"))
    return jax.shard_map(shards, mesh=mesh, in_specs=placed, out_specs=placed, check_vma=False)
```

```python
import functools

import jax
import jax.numpy as jnp
from jax import lax
from jax.experimental import pallas as pl
from jax.experimental.pallas import tpu as pltpu
from jax.sharding import PartitionSpec as P

ROUNDS = 2
FIRST_LIMIT = 56_400_000
STAT_ROWS = 136
TOLERANCE = 1e-7

Z_PAIR = {0: 1, 2: 3, 4: 5, 6: 7}
Z_FAR = ({0: 5, 1: 4, 2: 7, 3: 6}, {0: 2, 1: 3, 4: 6, 5: 7}, {0: 6, 1: 7, 2: 4, 3: 5})


def both_ways(pairs):
    return {**pairs, **{b: a for a, b in pairs.items()}}


def row_route(z_map=None, flip_x=False, flip_core=False):
    route = []
    for i in range(32):
        z, x, core = i // 4, i // 2 % 2, i % 2
        z = both_ways(z_map)[z] if z_map else z
        route.append((i, z * 4 + (x ^ flip_x) * 2 + (core ^ flip_core)))
    return route


def across(value, **kinds):
    return lax.ppermute(value, "row", row_route(**kinds))


def on_core_0(value, otherwise):
    return jnp.where(lax.axis_index("row") % 2 == 0, value, otherwise)


def from_three(value, single, first, second):
    route = [r for r in row_route(**single) if r[0] % 2 == 0] + [r for r in row_route(**first) if r[0] % 2]
    added = lax.ppermute(value, "row", route)
    more = lax.ppermute(value, "row", [r for r in row_route(**second) if r[0] % 2])
    return on_core_0(value, more) + added


def with_other_core(value):
    return value + across(value, flip_core=True)


def summed_over_rows(value):
    value = with_other_core(value)
    value = from_three(value, *(dict(z_map=pairs) for pairs in Z_FAR))
    value = with_other_core(value)
    value = from_three(value, dict(z_map=Z_PAIR, flip_x=True), dict(flip_x=True), dict(z_map=Z_PAIR))
    return value, across(value, flip_core=True)


def split(value):
    high = value.astype(jnp.bfloat16)
    return high, (value - high.astype(jnp.float32)).astype(jnp.bfloat16)


def contract(a, b, dims):
    (ah, al), (bh, bl) = a, b
    dot = functools.partial(lax.dot_general, dimension_numbers=(dims, ((), ())), preferred_element_type=jnp.float32)
    return dot(ah, bh) + (dot(al, bh) + dot(ah, bl))


def exact_dot(a, b, dims=((1,), (0,))):
    return lax.dot_general(
        a, b, dimension_numbers=(dims, ((), ())), precision=lax.Precision.HIGHEST, preferred_element_type=jnp.float32
    )


def partial_statistics(upper, lower):
    squares = [jnp.sum((v * v).reshape(-1, 8, v.shape[1]), axis=0) for v in (upper, lower)]
    return [contract(split(upper), split(lower), ((0,), (0,))), *squares]


def write_statistics(parts, out_ref):
    gram, *squares = parts
    width = gram.shape[0]
    out_ref[:width] = gram
    sums = [jnp.broadcast_to(jnp.sum(s, axis=0, keepdims=True), s.shape) for s in squares]
    is_upper = lax.broadcasted_iota(jnp.int32, sums[0].shape, 0) < 4
    out_ref[width:] = jnp.where(is_upper, *sums)


VMEM = pl.BlockSpec(memory_space=pltpu.VMEM)
HBM = pl.BlockSpec(memory_space=pltpu.HBM)
PARAMS = pltpu.CompilerParams(vmem_limit_bytes=8 << 20)
PIECES = 4


def pieces_of(rows):
    return [pl.ds(i * (rows // PIECES), rows // PIECES) for i in range(PIECES)]


def stat_shape(width):
    return jax.ShapeDtypeStruct((STAT_ROWS, width), jnp.float32)


def first_kernel(upper_hbm, lower_hbm, sums_ref, upper_ref, lower_ref, sems):
    copies = [
        pltpu.make_async_copy(source.at[rows], target.at[rows], sems.at[i, j])
        for j, rows in enumerate(pieces_of(upper_hbm.shape[0]))
        for i, (source, target) in enumerate(((upper_hbm, upper_ref), (lower_hbm, lower_ref)))
    ]
    for copy in copies:
        copy.start()
    for copy in copies:
        copy.wait()
    write_statistics(partial_statistics(upper_ref[...], lower_ref[...]), sums_ref)


def first_statistics(upper, lower):
    return pl.pallas_call(
        first_kernel,
        out_shape=stat_shape(upper.shape[1]),
        in_specs=[HBM, HBM],
        out_specs=VMEM,
        scratch_shapes=[pltpu.VMEM(upper.shape, jnp.float32)] * 2 + [pltpu.SemaphoreType.DMA((2, PIECES))],
        compiler_params=pltpu.CompilerParams(vmem_limit_bytes=FIRST_LIMIT),
        name="first_statistics",
    )(upper, lower)


def statistics_kernel(upper_ref, lower_ref, sums_ref):
    write_statistics(partial_statistics(upper_ref[...], lower_ref[...]), sums_ref)


def statistics(upper, lower):
    return pl.pallas_call(
        statistics_kernel,
        out_shape=stat_shape(upper.shape[1]),
        in_specs=[VMEM, VMEM],
        out_specs=VMEM,
        compiler_params=PARAMS,
        name="statistics",
    )(upper, lower)


def coupling_of(sums, row_total):
    width = sums.shape[1]
    sums = sums * (1.0 / row_total)
    cross_gram = sums[:width]
    upper_norms, lower_norms = sums[width : width + 1], sums[width + 4 : width + 5]
    upper_norms = jnp.broadcast_to(upper_norms, (width, width)).T
    gap = upper_norms - lower_norms
    both = upper_norms + lower_norms
    return -cross_gram * gap / (2.0 * gap * gap + 0.5 * both * both + 1e-05)


def scaled_residual(coupling):
    width = coupling.shape[0]
    identity = (
        lax.broadcasted_iota(jnp.int32, (width, width), 0) == lax.broadcasted_iota(jnp.int32, (width, width), 1)
    ).astype(jnp.float32)
    parts = split(coupling)
    outer = contract(parts, parts, ((1,), (1,)))
    size = jnp.sqrt(jnp.sum(jnp.sum(outer * outer, axis=0, keepdims=True), axis=1, keepdims=True))
    alpha = 2.0 / (2.0 + size)
    return (1.0 - alpha) * identity - alpha * outer, alpha, jnp.sum(size / (2.0 + size))


def two_factors(residual, right):
    parts = split(residual)
    right = right + contract(parts, split(right), ((1,), (0,)))
    square = contract(parts, parts, ((1,), (0,)))
    return right + contract(split(square), split(right), ((1,), (0,))), square


def solved(coupling, residual, alpha, bound, residual_ref, result_ref):
    def series(right):
        result_ref[...], residual_ref[...] = two_factors(residual, right)

        def factor(bound):
            square = exact_dot(residual_ref[...], residual_ref[...])
            residual_ref[...] = square
            result_ref[...] += exact_dot(square, result_ref[...])
            return bound * bound

        lax.while_loop(lambda bound: bound > TOLERANCE, factor, (bound * bound) * (bound * bound))

    series((2.0 * alpha) * coupling)

    @pl.when(bound > 0.5)
    def _():
        exact_outer = exact_dot(coupling, coupling, ((1,), (1,)))
        for _ in range(2):
            value = result_ref[...]
            series(alpha * ((2.0 * coupling - value) - exact_dot(exact_outer, value)))
            result_ref[...] += value

    return result_ref[...]


def with_rotation(sums, row_total, scratch, use):
    coupling = coupling_of(sums, row_total)
    residual, alpha, bound = scaled_residual(coupling)
    use(full_change(coupling, two_factors(residual, (2.0 * alpha) * coupling)[0]))

    @pl.when((bound * bound) * (bound * bound) > TOLERANCE)
    def _():
        use(full_change(coupling, solved(coupling, residual, alpha, bound, *scratch)))


def apply(upper, lower, change):
    return contract(split(jnp.concatenate([upper, lower], axis=1)), change, ((1,), (0,)))


def full_change(coupling, to_lower):
    both = (split(coupling), split(to_lower))
    upper_loss = contract(*both, ((1,), (1,)))
    lower_loss = contract(*both, ((0,), (0,)))
    return split(
        jnp.concatenate(
            [
                jnp.concatenate([-upper_loss, to_lower], axis=1),
                jnp.concatenate([-to_lower.T, -lower_loss], axis=1),
            ],
            axis=0,
        )
    )


def last_kernel(row_total, mine_ref, other_ref, upper_ref, lower_ref, upper_hbm, lower_hbm, residual_ref, result_ref,
                new_upper_ref, new_lower_ref, sems):
    width = upper_ref.shape[1]

    def use(change):
        copies = []
        for j, rows in enumerate(pieces_of(upper_ref.shape[0])):
            moved = apply(upper_ref[rows], lower_ref[rows], change)
            new_upper_ref[rows] = upper_ref[rows] + moved[:, :width]
            new_lower_ref[rows] = lower_ref[rows] + moved[:, width:]
            for i, (source, target) in enumerate(((new_upper_ref, upper_hbm), (new_lower_ref, lower_hbm))):
                copies.append(pltpu.make_async_copy(source.at[rows], target.at[rows], sems.at[i, j]))
                copies[-1].start()
        for copy in copies:
            copy.wait()

    with_rotation(mine_ref[...] + other_ref[...], row_total, (residual_ref, result_ref), use)


def rotated_last(mine, other, upper, lower, row_total):
    width = upper.shape[1]
    square = pltpu.VMEM((width, width), jnp.float32)
    return pl.pallas_call(
        functools.partial(last_kernel, row_total),
        out_shape=(jax.ShapeDtypeStruct(upper.shape, jnp.float32),) * 2,
        in_specs=[VMEM] * 4,
        out_specs=(HBM, HBM),
        scratch_shapes=[square, square]
        + [pltpu.VMEM(upper.shape, jnp.float32)] * 2
        + [pltpu.SemaphoreType.DMA((2, PIECES))],
        compiler_params=PARAMS,
        name="rotate_last",
    )(mine, other, upper, lower)


def rotate_kernel(row_total, mine_ref, other_ref, upper_ref, lower_ref, new_upper_ref, new_lower_ref, residual_ref, result_ref):
    width = upper_ref.shape[1]

    def use(change):
        moved = apply(upper_ref[...], lower_ref[...], change)
        new_upper_ref[...] = upper_ref[...] + moved[:, :width]
        new_lower_ref[...] = lower_ref[...] + moved[:, width:]

    with_rotation(mine_ref[...] + other_ref[...], row_total, (residual_ref, result_ref), use)


def rotated(mine, other, upper, lower, row_total):
    width = upper.shape[1]
    return pl.pallas_call(
        functools.partial(rotate_kernel, row_total),
        out_shape=(jax.ShapeDtypeStruct(upper.shape, jnp.float32),) * 2,
        in_specs=[VMEM] * 4,
        out_specs=(VMEM, VMEM),
        scratch_shapes=[pltpu.VMEM((width, width), jnp.float32)] * 2,
        compiler_params=PARAMS,
        name="rotate",
    )(mine, other, upper, lower)


def from_behind(block, distance):
    devices = lax.axis_size("col")
    return lax.ppermute(block, "col", [((i - distance) % devices, i) for i in range(devices)])


def shards(upper, lower):
    row_total = float(upper.shape[0] * lax.axis_size("row"))
    mine, other = summed_over_rows(first_statistics(upper, lower))
    upper, lower = rotated(mine, other, upper, lower, row_total)
    upper, lower = from_behind(upper, 1), from_behind(lower, -1)
    mine, other = summed_over_rows(statistics(upper, lower))
    return rotated_last(mine, other, upper, lower, row_total)


def solution(mesh):
    placed = (P("row", "col"), P("row", "col"))
    return jax.shard_map(shards, mesh=mesh, in_specs=placed, out_specs=placed, check_vma=False)
```
